512 devices in a mesh: dp: 32 (over z, x), block: 16 (over y, core).
Axes of the slice: x: 4, y: 8, z: 8, core: 2. Of those that a mesh axis runs over, the one named last changes fastest.
Arguments:
- gradient: float32 [1024, 16384], P('dp'), may hold values from -45 to 45
- left_root: float32 [16, 1024, 1024], P('block', 'dp'), may hold values from -0.1 to 4, as said below
- right_root: float32 [16, 1024, 1024], P('block', 'dp'), may hold values from -0.1 to 4, as said below
- first_moment: float32 [16, 1024, 1024], P('block', 'dp'), may hold values from -3 to 3
- second_moment: float32 [16, 1024, 1024], P('block', 'dp'), may hold values from 0.25 to 4
- step_count: int32 [1], replicated, may hold values from 1 to 40
- owner_table: int32 [16], replicated, may hold values from 0 to 15, each once
Outputs:
- update: float32 [1024, 16384], P('dp')
- first_new: float32 [16, 1024, 1024], P('block', 'dp')
- second_new: float32 [16, 1024, 1024], P('block', 'dp')
The draws below stay inside these ranges and needn't reach their ends.
Inputs may be any that keep to these rules, and one draw needn't show every extreme that they name: `left_root`: symmetric in its last two dimensions. `right_root`: symmetric in its last two dimensions.
All inputs are finite; a program needn't handle non-finite values.
Results may differ from the reference program's by a relative error of at most 0.000086.
Values sent between devices are 32-bit elements; how exact they have to be, the bound alone decides.
No kernel may reach another device: no remote copies, remote signals or barrier semaphores. Data moves between devices by JAX's collectives and lax.ppermute only.
A program may use at most 64 MiB of HBM per device.

```python
import math
import jax
import jax.numpy as jnp
from jax import lax

BS = 1024
NB = 16


def symmetric_block(key):
    key_off, key_diag = jax.random.split(key)
    raw_off = jnp.clip(jax.random.normal(key_off, (NB, BS, BS), jnp.float32), -4.0, 4.0)
    off_diag = (raw_off + jnp.swapaxes(raw_off, 1, 2)) * (0.45 / math.sqrt(2.0 * BS))
    off_diag = jnp.clip(off_diag, -0.1, 0.1)
    diag_values = jnp.exp(jax.random.uniform(key_diag, (NB, BS), jnp.float32, 0.0, math.log(3.0)))
    eye_mask = jnp.eye(BS, dtype=jnp.float32)
    return off_diag * (1.0 - eye_mask)[None] + diag_values[:, :, None] * eye_mask[None]


def draw_left_root(key, part):
    key = jax.random.fold_in(key, 11)
    return symmetric_block(key)


def draw_right_root(key, part):
    key = jax.random.fold_in(key, 23)
    return symmetric_block(key)


def draw_gradient(key, part):
    key = jax.random.fold_in(key, 37)
    key_noise, key_row, key_col = jax.random.split(key, 3)
    rising = jnp.exp(math.log(3.0) * jnp.arange(BS, dtype=jnp.float32) / BS)[:, None]
    row_scale = jnp.exp(jax.random.uniform(key_row, (BS, 1), jnp.float32, -0.6, 0.6))
    col_scale = jnp.exp(jax.random.uniform(key_col, (1, NB * BS), jnp.float32, -1.15, 1.15))
    noise_field = jnp.clip(jax.random.normal(key_noise, (BS, NB * BS), jnp.float32), -5.0, 5.0)
    return 0.5 * noise_field * rising * row_scale * col_scale


def shard_levels(own_key, extent, pieces, least, largest):
    def one(dim, parts):
        heights = jax.random.uniform(jax.random.fold_in(jax.random.fold_in(own_key, 6), dim), (parts,), jnp.float32, least / len(pieces), largest / len(pieces))
        return jnp.repeat(jnp.exp(heights), extent[dim] // parts).reshape((-1,) + (1,) * (len(extent) - dim - 1))

    level = one(*pieces[0])
    for cut in pieces[1:]:
        level = level * one(*cut)
    return level


def noise(stream_key, extent, spread, limit, pieces=(), kind=jnp.bfloat16):
    entries = jax.random.normal(stream_key, extent, jnp.float32) * spread
    if len(pieces) > 0:
        entries = shard_levels(stream_key, extent, pieces, -0.22, 0.18) * entries
    return jnp.clip(entries, min=-limit, max=limit).astype(kind)


def setup_inputs(seed: int = 0) -> dict:
    splits = jax.random.split(jax.random.key(seed), 8)
    gradient = draw_gradient(jax.random.fold_in(splits[7], 71), 0)
    left_root = draw_left_root(jax.random.fold_in(splits[7], 71), 0)
    right_root = draw_right_root(jax.random.fold_in(splits[7], 71), 0)
    first_moment = noise(splits[3], (NB, BS, BS), 0.5, 3.0, ((0, 16), (1, 32)), jnp.float32)
    second_moment = jnp.clip(jnp.exp(math.log(4.0) - 2.7725887 * jax.random.uniform(splits[4], (NB, BS, BS), jnp.float32) ** shard_levels(splits[4], (NB, BS, BS), ((0, 16), (1, 32)), -0.2, 0.2)), 0.25, 4.0)
    step_count = jax.random.randint(splits[5], (1,), 1, 41).astype(jnp.int32)
    owner_table = jax.random.permutation(splits[6], NB).astype(jnp.int32)
    return dict(gradient=gradient, left_root=left_root, right_root=right_root, first_moment=first_moment, second_moment=second_moment, step_count=step_count, owner_table=owner_table)


beta_one = 0.9
beta_two = 0.95
adam_eps = 1e-08
norm_eps = 1e-06

def reference(gradient, left_root, right_root, first_moment, second_moment, step_count, owner_table):
    blocks = jnp.transpose(gradient.reshape(BS, NB, BS), (1, 0, 2))
    positions = jnp.arange(NB, dtype=jnp.int32)
    matching = (owner_table[None, :] == positions[:, None]).astype(jnp.int32)
    chosen = lax.optimization_barrier(jnp.sum(matching * positions[None, :], axis=1)).astype(jnp.int32)
    owned_blocks = blocks[chosen]
    step_value = step_count[0].astype(jnp.float32)
    first_new = beta_one * first_moment + (1.0 - beta_one) * owned_blocks
    second_new = beta_two * second_moment + (1.0 - beta_two) * owned_blocks * owned_blocks
    first_fix = 1.0 - jnp.power(beta_one, step_value)
    second_fix = 1.0 - jnp.power(beta_two, step_value)
    adam_step = first_new / first_fix / (jnp.sqrt(second_new / second_fix) + adam_eps)
    right_side = jnp.matmul(owned_blocks, right_root, precision=lax.Precision.HIGHEST)
    precond = jnp.matmul(left_root, right_side, precision=lax.Precision.HIGHEST)
    adam_norm = jnp.sqrt(lax.optimization_barrier(jnp.sum(adam_step * adam_step, axis=(1, 2))))
    precond_norm = jnp.sqrt(lax.optimization_barrier(jnp.sum(precond * precond, axis=(1, 2))))
    graft_scale = adam_norm / (precond_norm + norm_eps)
    updates = graft_scale[:, None, None] * precond
    placed = updates[owner_table]
    update = jnp.transpose(placed, (1, 0, 2)).reshape(BS, NB * BS)
    return (update, first_new, second_new)
```

```python
import jax
import jax.numpy as jnp
from jax import lax
from jax.sharding import Mesh
from jax.sharding import PartitionSpec as P

beta_one = 0.9
beta_two = 0.95
adam_eps = 1e-08
norm_eps = 1e-06
HIGHEST = lax.Precision.HIGHEST


def gather_by_shifts(value, axis, count):
    me = lax.axis_index(axis)
    held = jnp.zeros((count,) + value.shape, value.dtype)
    for k in range(count):
        if k == 0:
            got = value
        else:
            got = lax.ppermute(value, axis, [(i, (i + k) % count) for i in range(count)])
        held = lax.dynamic_update_slice_in_dim(held, got[None], (me - k) % count, 0)
    return held


def gather_by_exchange(value, axes, count):
    return lax.all_to_all(
        jnp.broadcast_to(value[None], (count,) + value.shape), axes, 0, 0, tiled=True
    )


def local(gradient, left_root, right_root, first_moment, second_moment, step_count, owner_table):
    rows, width = left_root.shape[1], left_root.shape[2]
    blocks = owner_table.shape[0]
    quarters, near = lax.axis_size("q"), lax.axis_size("r") * lax.axis_size("x")
    ring = lax.axis_size("y")
    position = lax.axis_index("y") * 2 + lax.axis_index("core")
    chosen = jnp.sum(
        jnp.where(owner_table == position, jnp.arange(blocks, dtype=jnp.int32), 0)
    )
    grad = lax.dynamic_slice_in_dim(gradient, chosen * width, width, axis=1)

    grad_rows = gather_by_exchange(grad, ("r", "x"), near).reshape(near * rows, width)
    right_class = gather_by_shifts(right_root[0], "q", quarters).reshape(quarters * rows, width)

    step_value = step_count[0].astype(jnp.float32)
    first_new = beta_one * first_moment[0] + (1.0 - beta_one) * grad
    second_new = beta_two * second_moment[0] + (1.0 - beta_two) * grad * grad
    first_fix = 1.0 - jnp.power(beta_one, step_value)
    second_fix = 1.0 - jnp.power(beta_two, step_value)
    adam_step = first_new / first_fix / (jnp.sqrt(second_new / second_fix) + adam_eps)
    adam_sq = jnp.sum(adam_step * adam_step)

    right_side = lax.dot_general(
        grad_rows, right_class, (((1,), (1,)), ((), ())), precision=HIGHEST
    )
    left_rows = gather_by_exchange(left_root[0], ("r", "x"), near).reshape(near * rows, width)
    right_all = gather_by_shifts(right_side, "q", quarters).reshape(width, quarters * rows)
    precond = jnp.dot(left_rows, right_all, precision=HIGHEST)

    sums = jnp.stack([adam_sq, jnp.sum(precond * precond)])
    pieces = precond.reshape(near, rows, quarters * rows)
    tail = jnp.broadcast_to(
        jnp.pad(sums, (0, quarters * rows - 2))[None, None, :], (near, 8, quarters * rows)
    )
    sent = jnp.concatenate([pieces, tail], axis=1)
    got = lax.all_to_all(sent, ("r", "x"), 0, 0, tiled=True)
    mine = got[:, :rows].reshape(near, rows, quarters, rows)
    mine = jnp.transpose(mine, (1, 2, 0, 3)).reshape(rows, width)
    near_sums = jnp.sum(got[:, rows, :2], axis=0)

    own = gather_by_exchange(mine, "y", ring)
    totals = jnp.sum(lax.all_gather(near_sums, "q"), axis=0)
    scale = jnp.sqrt(totals[0]) / (jnp.sqrt(totals[1]) + norm_eps)
    scales = lax.all_gather(scale, ("y", "core"))
    other = lax.ppermute(own, "core", [(0, 1), (1, 0)])
    core = lax.axis_index("core")
    even = jnp.where(core == 0, own, other)
    odd = jnp.where(core == 0, other, own)
    both = jnp.stack([even, odd], axis=1).reshape(blocks, rows, width)
    placed = jnp.take(both, owner_table, axis=0) * jnp.take(scales, owner_table)[:, None, None]
    update = jnp.transpose(placed, (1, 0, 2)).reshape(rows, blocks * width)
    return update, first_new[None], second_new[None]


def solution(mesh):
    fine = Mesh(mesh.devices.reshape(4, 2, 4, 8, 2), ("q", "r", "x", "y", "core"))
    near, deep = ("q", "r", "x"), ("y", "core")
    flat, owned = P(near, None), P(deep, near, None)
    return jax.shard_map(
        local,
        mesh=fine,
        in_specs=(flat, owned, owned, owned, owned, P(), P()),
        out_specs=(flat, owned, owned),
        check_vma=False,
    )
```

```python
import functools

import jax
import jax.numpy as jnp
from jax import lax
from jax.experimental import pallas as pl
from jax.experimental.pallas import tpu as pltpu
from jax.sharding import Mesh
from jax.sharding import PartitionSpec as P

beta_one = 0.9
beta_two = 0.95
adam_eps = 1e-08
norm_eps = 1e-06
HIGHEST = lax.Precision.HIGHEST
GROUP = 4


def exchange(value, axes):
    return lax.all_to_all(value, axes, 0, 0, tiled=True)


def copies(value, count):
    return jnp.broadcast_to(value[None], (count,) + value.shape)


def place_kernel(spread, ring, rows, table, core, sums, own, other, out, scale):
    step = pl.program_id(0)

    @pl.when(step == 0)
    def _():
        total = jnp.sum(sums[...], axis=0)
        factor = jnp.sqrt(total[:, :, 0:1]) / (jnp.sqrt(total[:, :, 1:2]) + norm_eps)
        scale[...] = jnp.broadcast_to(factor.reshape(2 * ring, 1), scale.shape)

    lane = lax.broadcasted_iota(jnp.int32, (rows, 128), 1) // rows
    for k in range(GROUP):
        position = table[step * GROUP + k]
        deep = position // 2
        part = position - 2 * deep
        mine = part == core[0]
        factor = scale[pl.ds(part * ring + deep, 1), :]
        pieces = []
        for x in range(spread):
            held = own[x, deep, : 2 * rows, :]
            got = other[x, deep, : 2 * rows, :]
            pieces.append(jnp.where(mine, held, got) * factor)
        for z in range(ring):
            half, slot = z // 4, z % 4
            tile = jnp.zeros((rows, 128), jnp.float32)
            for x in range(spread):
                part_x = pieces[x][half * rows : (half + 1) * rows, :]
                if x != slot:
                    part_x = pltpu.roll(part_x, (x - slot) % 4 * rows, 1)
                tile = jnp.where(lane == x, part_x, tile)
            out[:, pl.ds(k * 1024 + z * 128, 128)] = tile


def place(table, core, sums, own, other, spread, ring, rows):
    blocks = table.shape[0]
    return pl.pallas_call(
        functools.partial(place_kernel, spread, ring, rows),
        out_shape=jax.ShapeDtypeStruct((rows, blocks * 1024), jnp.float32),
        grid_spec=pltpu.PrefetchScalarGridSpec(
            num_scalar_prefetch=2,
            grid=(blocks // GROUP,),
            in_specs=[
                pl.BlockSpec(sums.shape, lambda i, *_: (0, 0, 0, 0)),
                pl.BlockSpec(own.shape, lambda i, *_: (0, 0, 0, 0)),
                pl.BlockSpec(other.shape, lambda i, *_: (0, 0, 0, 0)),
            ],
            out_specs=pl.BlockSpec((rows, GROUP * 1024), lambda i, *_: (0, i)),
            scratch_shapes=[pltpu.VMEM((blocks, 128), jnp.float32)],
        ),
        compiler_params=pltpu.CompilerParams(vmem_limit_bytes=32 * 1024 * 1024),
        name="place",
    )(table, core, sums, own, other)


def local(gradient, left_root, right_root, first_moment, second_moment, step_count, owner_table):
    rows, width = left_root.shape[1], left_root.shape[2]
    blocks = owner_table.shape[0]
    deep, spread, ring = lax.axis_size("z"), lax.axis_size("x"), lax.axis_size("y")
    core = lax.axis_index("core")
    position = lax.axis_index("y") * 2 + core

    right_class = exchange(copies(right_root[0], deep), "z").reshape(deep * rows, width)

    chosen = jnp.sum(
        jnp.where(owner_table == position, jnp.arange(blocks, dtype=jnp.int32), 0)
    )
    grad = lax.dynamic_slice_in_dim(gradient, chosen * width, width, axis=1)
    grad_rows = lax.all_gather(grad, "x", axis=0, tiled=True)

    step_value = step_count[0].astype(jnp.float32)
    first_new = beta_one * first_moment[0] + (1.0 - beta_one) * grad
    second_new = beta_two * second_moment[0] + (1.0 - beta_two) * grad * grad
    first_fix = 1.0 - jnp.power(beta_one, step_value)
    second_fix = 1.0 - jnp.power(beta_two, step_value)
    adam_step = first_new / first_fix / (jnp.sqrt(second_new / second_fix) + adam_eps)
    adam_sq = jnp.sum(adam_step * adam_step)

    right_side = lax.dot_general(
        grad_rows, right_class, (((1,), (1,)), ((), ())), precision=HIGHEST
    )
    left_own, right_side = lax.optimization_barrier((left_root[0], right_side))
    left_rows = lax.all_gather(left_own, "x", axis=0, tiled=True)
    right_all = exchange(copies(right_side, deep), "z").reshape(width, deep * rows)
    precond = jnp.dot(left_rows, right_all, precision=HIGHEST)

    sums = jnp.stack([adam_sq, jnp.sum(precond * precond)])
    tail = jnp.broadcast_to(jnp.pad(sums, (0, 126))[None, None, :], (spread, 8, 128))
    pieces = jnp.transpose(precond.reshape(spread, rows, 2, 128), (0, 2, 1, 3))
    sent = jnp.concatenate([pieces.reshape(spread, 2 * rows, 128), tail], axis=1)
    sent = jnp.broadcast_to(sent[:, None], (spread, ring) + sent.shape[1:])
    own = exchange(sent.reshape(spread * ring, 2 * rows + 8, 128), ("x", "y"))
    other = lax.ppermute(own, "core", [(0, 1), (1, 0)])
    own = own.reshape(spread, ring, 2 * rows + 8, 128)
    other = other.reshape(spread, ring, 2 * rows + 8, 128)
    near = jnp.sum(own[:, :, 2 * rows, :], axis=0)
    totals = exchange(copies(near, deep * 2), ("z", "core")).reshape(deep, 2, ring, 128)
    update = place(
        owner_table, core.astype(jnp.int32)[None], totals, own, other, spread, ring, rows
    )
    return update, first_new[None], second_new[None]


def solution(mesh):
    fine = Mesh(mesh.devices.reshape(8, 4, 8, 2), ("z", "x", "y", "core"))
    near, deep = ("z", "x"), ("y", "core")
    flat, owned = P(near, None), P(deep, near, None)
    return jax.shard_map(
        local,
        mesh=fine,
        in_specs=(flat, owned, owned, owned, owned, P(), P()),
        out_specs=(flat, owned, owned),
        check_vma=False,
    )
```

```python
import functools

import jax
import jax.numpy as jnp
from jax import lax
from jax.experimental import pallas as pl
from jax.experimental.pallas import tpu as pltpu
from jax.sharding import Mesh
from jax.sharding import PartitionSpec as P

beta_one = 0.9
beta_two = 0.95
adam_eps = 1e-08
norm_eps = 1e-06
HIGHEST = lax.Precision.HIGHEST


def exchange(value, axes):
    return lax.all_to_all(value, axes, 0, 0, tiled=True)


def shifted(value, axis, by):
    count = lax.axis_size(axis)
    return lax.ppermute(value, axis, [(i, (i + by) % count) for i in range(count)])


def block_of(table, position, blocks):
    found = jnp.int32(0)
    for k in range(blocks):
        found += jnp.where(table[k] == position, k, 0)
    return found


def pick_kernel(blocks, table, position, gradient, out, arrived):
    width = out.shape[1]
    start = pl.multiple_of(block_of(table, position[0], blocks) * width, width)
    copy = pltpu.make_async_copy(gradient.at[:, pl.ds(start, width)], out, arrived)
    copy.start()
    copy.wait()


def pick(table, position, gradient, width):
    return pl.pallas_call(
        functools.partial(pick_kernel, table.shape[0]),
        out_shape=jax.ShapeDtypeStruct((gradient.shape[0], width), jnp.float32),
        in_specs=[
            pl.BlockSpec(memory_space=pltpu.SMEM),
            pl.BlockSpec(memory_space=pltpu.SMEM),
            pl.BlockSpec(memory_space=pl.ANY),
        ],
        out_specs=pl.BlockSpec(memory_space=pltpu.VMEM),
        scratch_shapes=[pltpu.SemaphoreType.DMA],
        name="pick",
    )(table, position, gradient)


def left_kernel(near, rows, left, right, adam, out):
    spread = near // 2
    tile = jnp.dot(
        left[...].reshape(near * rows, left.shape[-1]),
        right[...],
        precision=HIGHEST,
        preferred_element_type=jnp.float32,
    )
    lane = lax.broadcasted_iota(jnp.int32, (8, 128), 1)
    tail = jnp.where(lane == 0, adam[0, 0], jnp.where(lane == 1, jnp.sum(tile * tile), 0.0))
    for x in range(spread):
        for r in range(2):
            at = (x * 2 + r) * rows
            out[r * spread + x, :rows, :] = tile[at : at + rows, :]
            out[r * spread + x, rows:, :] = tail


def left_multiply(left, right, adam, near, rows):
    return pl.pallas_call(
        functools.partial(left_kernel, near, rows),
        out_shape=jax.ShapeDtypeStruct((near, rows + 8, 128), jnp.float32),
        in_specs=[
            pl.BlockSpec(memory_space=pltpu.VMEM),
            pl.BlockSpec(memory_space=pltpu.VMEM),
            pl.BlockSpec(memory_space=pltpu.SMEM),
        ],
        out_specs=pl.BlockSpec(memory_space=pltpu.VMEM),
        compiler_params=pltpu.CompilerParams(vmem_limit_bytes=32 * 1024 * 1024),
        name="left_multiply",
    )(left, right, adam)


def scale_kernel(near, rows, held, sums, out):
    total = jnp.sum(sums[...], axis=0, keepdims=True)
    factor = jnp.sqrt(total[:, 0:1]) / (jnp.sqrt(total[:, 1:2]) + norm_eps)
    for k in range(near):
        piece = held[k, :rows, :] * factor
        for y in range(out.shape[0]):
            out[y, k * rows : (k + 1) * rows, :] = piece


def scale_copies(held, sums, near, rows, ring):
    return pl.pallas_call(
        functools.partial(scale_kernel, near, rows),
        out_shape=jax.ShapeDtypeStruct((ring, near * rows, 128), jnp.float32),
        in_specs=[pl.BlockSpec(memory_space=pltpu.VMEM)] * 2,
        out_specs=pl.BlockSpec(memory_space=pltpu.VMEM),
        compiler_params=pltpu.CompilerParams(vmem_limit_bytes=32 * 1024 * 1024),
        name="scale_copies",
    )(held, sums)


def place_kernel(quarters, spread, rows, blocks, table, part, held, *rest):
    out, tiles, sent = rest[-3:]
    lane = lax.broadcasted_iota(jnp.int32, (rows, 128), 1) // rows
    copies_out = []
    for y in range(held.shape[0]):
        for r in range(2):
            pieces = []
            for x in range(spread):
                at = (r * spread + x) * rows
                pieces.append(held[y, at : at + rows, :])
            for q in range(quarters):
                tile = pieces[q]
                for x in range(spread):
                    if x != q:
                        turned = pltpu.roll(pieces[x], (x - q) % 4 * rows, 1)
                        tile = jnp.where(lane == x, turned, tile)
                at = q * 256 + r * 128
                tiles[y, :, at : at + 128] = tile
        width = tiles.shape[2]
        start = pl.multiple_of(block_of(table, 2 * y + part[0], blocks) * width, width)
        copy = pltpu.make_async_copy(tiles.at[y], out.at[:, pl.ds(start, width)], sent.at[y])
        copy.start()
        copies_out.append(copy)
    for copy in copies_out:
        copy.wait()


def place(table, part, held, update, quarters, spread, rows, width):
    blocks, ring = table.shape[0], held.shape[0]
    operands = [table, part, held] + ([] if update is None else [update])
    return pl.pallas_call(
        functools.partial(place_kernel, quarters, spread, rows, blocks),
        out_shape=jax.ShapeDtypeStruct((rows, blocks * width), jnp.float32),
        in_specs=[
            pl.BlockSpec(memory_space=pltpu.SMEM),
            pl.BlockSpec(memory_space=pltpu.SMEM),
            pl.BlockSpec(memory_space=pltpu.VMEM),
        ]
        + ([] if update is None else [pl.BlockSpec(memory_space=pl.ANY)]),
        out_specs=pl.BlockSpec(memory_space=pl.ANY),
        scratch_shapes=[
            pltpu.VMEM((ring, rows, width), jnp.float32),
            pltpu.SemaphoreType.DMA((ring,)),
        ],
        input_output_aliases={} if update is None else {3: 0},
        compiler_params=pltpu.CompilerParams(vmem_limit_bytes=32 * 1024 * 1024),
        cost_estimate=pl.CostEstimate(flops=0, bytes_accessed=2 * ring * rows * width * 4, transcendentals=0),
        name="place_own" if update is None else "place_other",
    )(*operands)


def local(gradient, left_root, right_root, first_moment, second_moment, step_count, owner_table):
    rows, width = left_root.shape[1], left_root.shape[2]
    quarters, spread, ring = lax.axis_size("q"), lax.axis_size("x"), lax.axis_size("y")
    near = 2 * spread
    core = lax.axis_index("core").astype(jnp.int32)
    position = lax.axis_index("y").astype(jnp.int32) * 2 + core
    is_own = (jnp.arange(2, dtype=jnp.int32) == lax.axis_index("r"))[None, :, None, None]

    def spread_pair(value, got):
        shape = (spread, 2) + value.shape
        return jnp.where(
            jnp.broadcast_to(is_own, shape),
            jnp.broadcast_to(value, shape),
            jnp.broadcast_to(got, shape),
        )

    grad = pick(owner_table, position[None], gradient, width)
    grad_pair = spread_pair(grad, shifted(grad, "r", 1))
    grad_rows = exchange(grad_pair, "x")
    grad_rows = jnp.transpose(grad_rows, (1, 0, 2, 3)).reshape(near * rows, width)
    right_class = lax.all_gather(right_root[0], "q", axis=0, tiled=True)

    step_value = step_count[0].astype(jnp.float32)
    first_new = beta_one * first_moment[0] + (1.0 - beta_one) * grad
    second_new = beta_two * second_moment[0] + (1.0 - beta_two) * grad * grad
    first_fix = 1.0 - jnp.power(beta_one, step_value)
    second_fix = 1.0 - jnp.power(beta_two, step_value)
    adam_step = first_new / first_fix / (jnp.sqrt(second_new / second_fix) + adam_eps)
    adam_sq = jnp.sum(adam_step * adam_step)

    left_pair = spread_pair(left_root[0], shifted(left_root[0], "r", 1))
    left_pair, grad_rows, right_class = lax.optimization_barrier(
        (left_pair, grad_rows, right_class)
    )
    left_rows = exchange(left_pair, "x")
    right_side = lax.dot_general(
        grad_rows, right_class, (((1,), (1,)), ((), ())), precision=HIGHEST
    )
    right_all = lax.all_gather(right_side, "q", axis=0, tiled=True)
    sent = left_multiply(left_rows, right_all, adam_sq.reshape(1, 1), near, rows)
    got = exchange(sent, ("r", "x"))
    near_sums = jnp.sum(got[:, rows, :], axis=0, keepdims=True)
    totals = lax.all_gather(near_sums, "q", axis=0, tiled=True)
    own = exchange(scale_copies(got, totals, near, rows, ring), "y")
    other = lax.ppermute(own, "core", [(0, 1), (1, 0)])
    update = place(owner_table, core[None], own, None, quarters, spread, rows, width)
    update = place(owner_table, 1 - core[None], other, update, quarters, spread, rows, width)
    return update, first_new[None], second_new[None]


def solution(mesh):
    fine = Mesh(mesh.devices.reshape(4, 2, 4, 8, 2), ("q", "r", "x", "y", "core"))
    near, deep = ("q", "r", "x"), ("y", "core")
    flat, owned = P(near, None), P(deep, near, None)
    return jax.shard_map(
        local,
        mesh=fine,
        in_specs=(flat, owned, owned, owned, owned, P(), P()),
        out_specs=(flat, owned, owned),
        check_vma=False,
    )
```

```python
import functools

import jax
import jax.numpy as jnp
from jax import lax
from jax.experimental import pallas as pl
from jax.experimental.pallas import tpu as pltpu
from jax.sharding import Mesh
from jax.sharding import PartitionSpec as P

beta_one = 0.9
beta_two = 0.95
adam_eps = 1e-08
norm_eps = 1e-06
HIGHEST = lax.Precision.HIGHEST


def exchange(value, axes):
    return lax.all_to_all(value, axes, 0, 0, tiled=True)


def shifted(value, axis, by):
    count = lax.axis_size(axis)
    return lax.ppermute(value, axis, [(i, (i + by) % count) for i in range(count)])


def block_of(table, position, blocks):
    found = jnp.int32(0)
    for k in range(blocks):
        found += jnp.where(table[k] == position, k, 0)
    return found


def pick_kernel(blocks, table, position, gradient, out, arrived):
    width = out.shape[1]
    start = pl.multiple_of(block_of(table, position[0], blocks) * width, width)
    copy = pltpu.make_async_copy(gradient.at[:, pl.ds(start, width)], out, arrived)
    copy.start()
    copy.wait()


def pick(table, position, gradient, width):
    return pl.pallas_call(
        functools.partial(pick_kernel, table.shape[0]),
        out_shape=jax.ShapeDtypeStruct((gradient.shape[0], width), jnp.float32),
        in_specs=[
            pl.BlockSpec(memory_space=pltpu.SMEM),
            pl.BlockSpec(memory_space=pltpu.SMEM),
            pl.BlockSpec(memory_space=pl.ANY),
        ],
        out_specs=pl.BlockSpec(memory_space=pltpu.VMEM),
        scratch_shapes=[pltpu.SemaphoreType.DMA],
        name="pick",
    )(table, position, gradient)


def left_kernel(near, rows, left, right, adam, out):
    spread = near // 2
    tile = jnp.dot(
        left[...].reshape(near * rows, left.shape[-1]),
        right[...],
        precision=HIGHEST,
        preferred_element_type=jnp.float32,
    )
    lane = lax.broadcasted_iota(jnp.int32, (8, 128), 1)
    tail = jnp.where(lane == 0, adam[0, 0], jnp.where(lane == 1, jnp.sum(tile * tile), 0.0))
    for x in range(spread):
        for r in range(2):
            at = (x * 2 + r) * rows
            out[r * spread + x, :rows, :] = tile[at : at + rows, :]
            out[r * spread + x, rows:, :] = tail


def left_multiply(left, right, adam, near, rows):
    return pl.pallas_call(
        functools.partial(left_kernel, near, rows),
        out_shape=jax.ShapeDtypeStruct((near, rows + 8, 128), jnp.float32),
        in_specs=[
            pl.BlockSpec(memory_space=pltpu.VMEM),
            pl.BlockSpec(memory_space=pltpu.VMEM),
            pl.BlockSpec(memory_space=pltpu.SMEM),
        ],
        out_specs=pl.BlockSpec(memory_space=pltpu.VMEM),
        compiler_params=pltpu.CompilerParams(vmem_limit_bytes=32 * 1024 * 1024),
        name="left_multiply",
    )(left, right, adam)


def scale_kernel(quarters, spread, rows, held, sums, out):
    total = jnp.sum(sums[...], axis=0, keepdims=True)
    factor = jnp.sqrt(total[:, 0:1]) / (jnp.sqrt(total[:, 1:2]) + norm_eps)
    lane = lax.broadcasted_iota(jnp.int32, (rows, 128), 1) // rows
    for r in range(2):
        pieces = [held[r * spread + x, :rows, :] * factor for x in range(spread)]
        for q in range(quarters):
            tile = pieces[q]
            for x in range(spread):
                if x != q:
                    turned = pltpu.roll(pieces[x], (x - q) % 4 * rows, 1)
                    tile = jnp.where(lane == x, turned, tile)
            at = (q * 2 + r) * 128
            for y in range(out.shape[0]):
                out[y, :, at : at + 128] = tile


def scale_copies(held, sums, quarters, spread, rows, ring, width):
    return pl.pallas_call(
        functools.partial(scale_kernel, quarters, spread, rows),
        out_shape=jax.ShapeDtypeStruct((ring, rows, width), jnp.float32),
        in_specs=[pl.BlockSpec(memory_space=pltpu.VMEM)] * 2,
        out_specs=pl.BlockSpec(memory_space=pltpu.VMEM),
        compiler_params=pltpu.CompilerParams(vmem_limit_bytes=32 * 1024 * 1024),
        name="scale_copies",
    )(held, sums)


def place_kernel(blocks, table, part, held, *rest):
    out, sent = rest[-2:]
    width = held.shape[2]
    started = []
    for y in range(held.shape[0]):
        start = pl.multiple_of(block_of(table, 2 * y + part[0], blocks) * width, width)
        copy = pltpu.make_async_copy(held.at[y], out.at[:, pl.ds(start, width)], sent.at[y])
        copy.start()
        started.append(copy)
    for copy in started:
        copy.wait()


def place(table, part, held, update):
    blocks = table.shape[0]
    ring, rows, width = held.shape
    operands = [table, part, held] + ([] if update is None else [update])
    return pl.pallas_call(
        functools.partial(place_kernel, blocks),
        out_shape=jax.ShapeDtypeStruct((rows, blocks * width), jnp.float32),
        in_specs=[
            pl.BlockSpec(memory_space=pltpu.SMEM),
            pl.BlockSpec(memory_space=pltpu.SMEM),
            pl.BlockSpec(memory_space=pltpu.VMEM),
        ]
        + ([] if update is None else [pl.BlockSpec(memory_space=pl.ANY)]),
        out_specs=pl.BlockSpec(memory_space=pl.ANY),
        scratch_shapes=[pltpu.SemaphoreType.DMA((ring,))],
        input_output_aliases={} if update is None else {3: 0},
        compiler_params=pltpu.CompilerParams(vmem_limit_bytes=32 * 1024 * 1024),
        cost_estimate=pl.CostEstimate(
            flops=0, bytes_accessed=2 * ring * rows * width * 4, transcendentals=0
        ),
        name="place_own" if update is None else "place_other",
    )(*operands)


def local(gradient, left_root, right_root, first_moment, second_moment, step_count, owner_table):
    rows, width = left_root.shape[1], left_root.shape[2]
    quarters, spread, ring = lax.axis_size("q"), lax.axis_size("x"), lax.axis_size("y")
    near = 2 * spread
    core = lax.axis_index("core").astype(jnp.int32)
    position = lax.axis_index("y").astype(jnp.int32) * 2 + core
    is_own = (jnp.arange(2, dtype=jnp.int32) == lax.axis_index("r"))[None, :, None, None]

    def spread_pair(value, got):
        shape = (spread, 2) + value.shape
        return jnp.where(
            jnp.broadcast_to(is_own, shape),
            jnp.broadcast_to(value, shape),
            jnp.broadcast_to(got, shape),
        )

    grad = pick(owner_table, position[None], gradient, width)
    grad_pair = spread_pair(grad, shifted(grad, "r", 1))
    right_class = lax.all_gather(right_root[0], "q", axis=0, tiled=True)

    step_value = step_count[0].astype(jnp.float32)
    first_new = beta_one * first_moment[0] + (1.0 - beta_one) * grad
    second_new = beta_two * second_moment[0] + (1.0 - beta_two) * grad * grad
    first_fix = 1.0 - jnp.power(beta_one, step_value)
    second_fix = 1.0 - jnp.power(beta_two, step_value)
    adam_step = first_new / first_fix / (jnp.sqrt(second_new / second_fix) + adam_eps)
    adam_sq = jnp.sum(adam_step * adam_step)

    grad_pair, adam_sq = lax.optimization_barrier((grad_pair, adam_sq))
    grad_rows = exchange(grad_pair, "x")
    grad_rows = jnp.transpose(grad_rows, (1, 0, 2, 3)).reshape(near * rows, width)
    left_pair = spread_pair(left_root[0], shifted(left_root[0], "r", 1))
    left_pair, grad_rows, right_class = lax.optimization_barrier(
        (left_pair, grad_rows, right_class)
    )
    left_rows = exchange(left_pair, "x")
    right_side = lax.dot_general(
        grad_rows, right_class, (((1,), (1,)), ((), ())), precision=HIGHEST
    )
    right_all = lax.all_gather(right_side, "q", axis=0, tiled=True)
    sent = left_multiply(left_rows, right_all, adam_sq.reshape(1, 1), near, rows)
    got = exchange(sent, ("r", "x"))
    near_sums = jnp.sum(got[:, rows, :], axis=0, keepdims=True)
    totals = lax.all_gather(near_sums, "q", axis=0, tiled=True)
    own = exchange(scale_copies(got, totals, quarters, spread, rows, ring, width), "y")
    other = lax.ppermute(own, "core", [(0, 1), (1, 0)])
    update = place(owner_table, core[None], own, None)
    update = place(owner_table, 1 - core[None], other, update)
    return update, first_new[None], second_new[None]


def solution(mesh):
    fine = Mesh(mesh.devices.reshape(4, 2, 4, 8, 2), ("q", "r", "x", "y", "core"))
    near, deep = ("q", "r", "x"), ("y", "core")
    flat, owned = P(near, None), P(deep, near, None)
    return jax.shard_map(
        local,
        mesh=fine,
        in_specs=(flat, owned, owned, owned, owned, P(), P()),
        out_specs=(flat, owned, owned),
        check_vma=False,
    )
```

```python
import functools

import jax
import jax.numpy as jnp
from jax import lax
from jax.experimental import pallas as pl
from jax.experimental.pallas import tpu as pltpu
from jax.sharding import Mesh
from jax.sharding import PartitionSpec as P

beta_one = 0.9
beta_two = 0.95
adam_eps = 1e-08
norm_eps = 1e-06
HIGHEST = lax.Precision.HIGHEST


def exchange(value, axes):
    return lax.all_to_all(value, axes, 0, 0, tiled=True)


def shifted(value, axis, by):
    count = lax.axis_size(axis)
    return lax.ppermute(value, axis, [(i, (i + by) % count) for i in range(count)])


def block_of(table, position, blocks):
    found = jnp.int32(0)
    for k in range(blocks):
        found += jnp.where(table[k] == position, k, 0)
    return found


def pick_kernel(blocks, table, position, gradient, out, arrived):
    width = out.shape[1]
    start = pl.multiple_of(block_of(table, position[0], blocks) * width, width)
    copy = pltpu.make_async_copy(gradient.at[:, pl.ds(start, width)], out, arrived)
    copy.start()
    copy.wait()


def pick(table, position, gradient, width):
    return pl.pallas_call(
        functools.partial(pick_kernel, table.shape[0]),
        out_shape=jax.ShapeDtypeStruct((gradient.shape[0], width), jnp.float32),
        in_specs=[
            pl.BlockSpec(memory_space=pltpu.SMEM),
            pl.BlockSpec(memory_space=pltpu.SMEM),
            pl.BlockSpec(memory_space=pl.ANY),
        ],
        out_specs=pl.BlockSpec(memory_space=pltpu.VMEM),
        scratch_shapes=[pltpu.SemaphoreType.DMA],
        name="pick",
    )(table, position, gradient)


def left_kernel(near, rows, left, right, adam, out):
    spread = near // 2
    tile = jnp.dot(
        left[...].reshape(near * rows, left.shape[-1]),
        right[...],
        precision=HIGHEST,
        preferred_element_type=jnp.float32,
    )
    lane = lax.broadcasted_iota(jnp.int32, (8, 128), 1)
    tail = jnp.where(lane == 0, adam[0, 0], jnp.where(lane == 1, jnp.sum(tile * tile), 0.0))
    for x in range(spread):
        for r in range(2):
            at = (x * 2 + r) * rows
            out[r * spread + x, :rows, :] = tile[at : at + rows, :]
            out[r * spread + x, rows:, :] = tail


def left_multiply(left, right, adam, near, rows):
    return pl.pallas_call(
        functools.partial(left_kernel, near, rows),
        out_shape=jax.ShapeDtypeStruct((near, rows + 8, 128), jnp.float32),
        in_specs=[
            pl.BlockSpec(memory_space=pltpu.VMEM),
            pl.BlockSpec(memory_space=pltpu.VMEM),
            pl.BlockSpec(memory_space=pltpu.SMEM),
        ],
        out_specs=pl.BlockSpec(memory_space=pltpu.VMEM),
        compiler_params=pltpu.CompilerParams(vmem_limit_bytes=32 * 1024 * 1024),
        name="left_multiply",
    )(left, right, adam)


def order_kernel(quarters, spread, rows, held, out):
    lane = lax.broadcasted_iota(jnp.int32, (rows, 128), 1) // rows
    for r in range(2):
        pieces = [held[r * spread + x, :rows, :] for x in range(spread)]
        for q in range(quarters):
            tile = pieces[q]
            for x in range(spread):
                if x != q:
                    turned = pltpu.roll(pieces[x], (x - q) % 4 * rows, 1)
                    tile = jnp.where(lane == x, turned, tile)
            at = (q * 2 + r) * 128
            for y in range(out.shape[0]):
                out[y, :, at : at + 128] = tile


def order_copies(held, quarters, spread, rows, ring, width):
    return pl.pallas_call(
        functools.partial(order_kernel, quarters, spread, rows),
        out_shape=jax.ShapeDtypeStruct((ring, rows, width), jnp.float32),
        in_specs=[pl.BlockSpec(memory_space=pltpu.VMEM)],
        out_specs=pl.BlockSpec(memory_space=pltpu.VMEM),
        compiler_params=pltpu.CompilerParams(vmem_limit_bytes=32 * 1024 * 1024),
        name="order_copies",
    )(held)


def place_kernel(blocks, table, part, sums, held, *rest):
    out, tiles, sent = rest[-3:]
    width = held.shape[2]
    started = []
    for y in range(held.shape[0]):
        total = sums[pl.ds(2 * y + part[0], 1), :]
        factor = jnp.sqrt(total[:, 0:1]) / (jnp.sqrt(total[:, 1:2]) + norm_eps)
        tiles[y] = held[y] * factor
        start = pl.multiple_of(block_of(table, 2 * y + part[0], blocks) * width, width)
        copy = pltpu.make_async_copy(tiles.at[y], out.at[:, pl.ds(start, width)], sent.at[y])
        copy.start()
        started.append(copy)
    for copy in started:
        copy.wait()


def place(table, part, sums, held, update):
    blocks = table.shape[0]
    ring, rows, width = held.shape
    operands = [table, part, sums, held] + ([] if update is None else [update])
    return pl.pallas_call(
        functools.partial(place_kernel, blocks),
        out_shape=jax.ShapeDtypeStruct((rows, blocks * width), jnp.float32),
        in_specs=[
            pl.BlockSpec(memory_space=pltpu.SMEM),
            pl.BlockSpec(memory_space=pltpu.SMEM),
            pl.BlockSpec(memory_space=pltpu.VMEM),
            pl.BlockSpec(memory_space=pltpu.VMEM),
        ]
        + ([] if update is None else [pl.BlockSpec(memory_space=pl.ANY)]),
        out_specs=pl.BlockSpec(memory_space=pl.ANY),
        scratch_shapes=[
            pltpu.VMEM((ring, rows, width), jnp.float32),
            pltpu.SemaphoreType.DMA((ring,)),
        ],
        input_output_aliases={} if update is None else {4: 0},
        compiler_params=pltpu.CompilerParams(vmem_limit_bytes=32 * 1024 * 1024),
        cost_estimate=pl.CostEstimate(
            flops=0, bytes_accessed=2 * ring * rows * width * 4, transcendentals=0
        ),
        name="place_own" if update is None else "place_other",
    )(*operands)


def local(gradient, left_root, right_root, first_moment, second_moment, step_count, owner_table):
    rows, width = left_root.shape[1], left_root.shape[2]
    quarters, spread, ring = lax.axis_size("q"), lax.axis_size("x"), lax.axis_size("y")
    near = 2 * spread
    core = lax.axis_index("core").astype(jnp.int32)
    position = lax.axis_index("y").astype(jnp.int32) * 2 + core
    is_own = (jnp.arange(2, dtype=jnp.int32) == lax.axis_index("r"))[None, :, None, None]

    def spread_pair(value, got):
        shape = (spread, 2) + value.shape
        return jnp.where(
            jnp.broadcast_to(is_own, shape),
            jnp.broadcast_to(value, shape),
            jnp.broadcast_to(got, shape),
        )

    grad = pick(owner_table, position[None], gradient, width)
    grad_pair = spread_pair(grad, shifted(grad, "r", 1))
    right_class = lax.all_gather(right_root[0], "q", axis=0, tiled=True)

    step_value = step_count[0].astype(jnp.float32)
    first_new = beta_one * first_moment[0] + (1.0 - beta_one) * grad
    second_new = beta_two * second_moment[0] + (1.0 - beta_two) * grad * grad
    first_fix = 1.0 - jnp.power(beta_one, step_value)
    second_fix = 1.0 - jnp.power(beta_two, step_value)
    adam_step = first_new / first_fix / (jnp.sqrt(second_new / second_fix) + adam_eps)
    adam_sq = jnp.sum(adam_step * adam_step)

    left_got = shifted(left_root[0], "r", 1)
    grad_pair, left_got, adam_sq = lax.optimization_barrier((grad_pair, left_got, adam_sq))
    grad_rows = exchange(grad_pair, "x")
    grad_rows = jnp.transpose(grad_rows, (1, 0, 2, 3)).reshape(near * rows, width)
    left_pair = spread_pair(left_root[0], left_got)
    left_pair, grad_rows, right_class = lax.optimization_barrier(
        (left_pair, grad_rows, right_class)
    )
    left_rows = exchange(left_pair, "x")
    right_side = lax.dot_general(
        grad_rows, right_class, (((1,), (1,)), ((), ())), precision=HIGHEST
    )
    right_all = lax.all_gather(right_side, "q", axis=0, tiled=True)
    sent = left_multiply(left_rows, right_all, adam_sq.reshape(1, 1), near, rows)
    got = exchange(sent, ("r", "x"))
    near_sums = jnp.sum(got[:, rows, :], axis=0, keepdims=True)
    totals = lax.all_gather(near_sums, "q", axis=0, tiled=True)
    own = exchange(order_copies(got, quarters, spread, rows, ring, width), "y")
    totals = jnp.sum(totals, axis=0, keepdims=True)
    all_sums = lax.all_gather(totals, ("y", "core"), axis=0, tiled=True)
    own, all_sums = lax.optimization_barrier((own, all_sums))
    other = lax.ppermute(own, "core", [(0, 1), (1, 0)])
    update = place(owner_table, core[None], all_sums, own, None)
    update = place(owner_table, 1 - core[None], all_sums, other, update)
    return update, first_new[None], second_new[None]


def solution(mesh):
    fine = Mesh(mesh.devices.reshape(4, 2, 4, 8, 2), ("q", "r", "x", "y", "core"))
    near, deep = ("q", "r", "x"), ("y", "core")
    flat, owned = P(near, None), P(deep, near, None)
    return jax.shard_map(
        local,
        mesh=fine,
        in_specs=(flat, owned, owned, owned, owned, P(), P()),
        out_specs=(flat, owned, owned),
        check_vma=False,
    )
```

```python
import functools

import jax
import jax.numpy as jnp
from jax import lax
from jax.experimental import pallas as pl
from jax.experimental.pallas import tpu as pltpu
from jax.sharding import Mesh
from jax.sharding import PartitionSpec as P

beta_one = 0.9
beta_two = 0.95
adam_eps = 1e-08
norm_eps = 1e-06
HIGHEST = lax.Precision.HIGHEST


def exchange(value, axes):
    return lax.all_to_all(value, axes, 0, 0, tiled=True)


def shifted(value, axis, by):
    count = lax.axis_size(axis)
    return lax.ppermute(value, axis, [(i, (i + by) % count) for i in range(count)])


def block_of(table, position, blocks):
    found = jnp.int32(0)
    for k in range(blocks):
        found += jnp.where(table[k] == position, k, 0)
    return found


def pick_kernel(blocks, table, gradient, out, arrived):
    width = out.shape[1]
    position = lax.axis_index("y") * 2 + lax.axis_index("core")
    start = pl.multiple_of(block_of(table, position, blocks) * width, width)
    copy = pltpu.make_async_copy(gradient.at[:, pl.ds(start, width)], out, arrived)
    copy.start()
    copy.wait()


def pick(table, gradient, width):
    return pl.pallas_call(
        functools.partial(pick_kernel, table.shape[0]),
        out_shape=jax.ShapeDtypeStruct((gradient.shape[0], width), jnp.float32),
        in_specs=[
            pl.BlockSpec(memory_space=pltpu.SMEM),
            pl.BlockSpec(memory_space=pl.ANY),
        ],
        out_specs=pl.BlockSpec(memory_space=pltpu.VMEM),
        scratch_shapes=[pltpu.SemaphoreType.DMA],
        name="pick",
    )(table, gradient)


def left_kernel(near, rows, left, right, adam, out):
    spread = near // 2
    tile = jnp.dot(
        left[...].reshape(near * rows, left.shape[-1]),
        right[...],
        precision=HIGHEST,
        preferred_element_type=jnp.float32,
    )
    lane = lax.broadcasted_iota(jnp.int32, (8, 128), 1)
    tail = jnp.where(lane == 0, adam[0, 0], jnp.where(lane == 1, jnp.sum(tile * tile), 0.0))
    for x in range(spread):
        for r in range(2):
            at = (x * 2 + r) * rows
            out[r * spread + x, :rows, :] = tile[at : at + rows, :]
            out[r * spread + x, rows:, :] = tail


def left_multiply(left, right, adam, near, rows):
    return pl.pallas_call(
        functools.partial(left_kernel, near, rows),
        out_shape=jax.ShapeDtypeStruct((near, rows + 8, 128), jnp.float32),
        in_specs=[
            pl.BlockSpec(memory_space=pltpu.VMEM),
            pl.BlockSpec(memory_space=pltpu.VMEM),
            pl.BlockSpec(memory_space=pltpu.SMEM),
        ],
        out_specs=pl.BlockSpec(memory_space=pltpu.VMEM),
        compiler_params=pltpu.CompilerParams(vmem_limit_bytes=32 * 1024 * 1024),
        name="left_multiply",
    )(left, right, adam)


def order_kernel(quarters, spread, rows, held, out):
    lane = lax.broadcasted_iota(jnp.int32, (rows, 128), 1) // rows
    for r in range(2):
        pieces = [held[r * spread + x, :rows, :] for x in range(spread)]
        for q in range(quarters):
            tile = pieces[q]
            for x in range(spread):
                if x != q:
                    turned = pltpu.roll(pieces[x], (x - q) % 4 * rows, 1)
                    tile = jnp.where(lane == x, turned, tile)
            at = (q * 2 + r) * 128
            for y in range(out.shape[0]):
                out[y, :, at : at + 128] = tile


def order_copies(held, quarters, spread, rows, ring, width):
    return pl.pallas_call(
        functools.partial(order_kernel, quarters, spread, rows),
        out_shape=jax.ShapeDtypeStruct((ring, rows, width), jnp.float32),
        in_specs=[pl.BlockSpec(memory_space=pltpu.VMEM)],
        out_specs=pl.BlockSpec(memory_space=pltpu.VMEM),
        compiler_params=pltpu.CompilerParams(vmem_limit_bytes=32 * 1024 * 1024),
        name="order_copies",
    )(held)


def place_kernel(blocks, table, sums, held, *rest):
    out, tiles, sent = rest[-3:]
    core = lax.axis_index("core")
    part = core if len(rest) == 3 else 1 - core
    width = held.shape[2]
    started = []
    for y in range(held.shape[0]):
        total = sums[pl.ds(2 * y + part, 1), :]
        factor = jnp.sqrt(total[:, 0:1]) / (jnp.sqrt(total[:, 1:2]) + norm_eps)
        tiles[y] = held[y] * factor
        start = pl.multiple_of(block_of(table, 2 * y + part, blocks) * width, width)
        copy = pltpu.make_async_copy(tiles.at[y], out.at[:, pl.ds(start, width)], sent.at[y])
        copy.start()
        started.append(copy)
    for copy in started:
        copy.wait()


def place(table, sums, held, update):
    blocks = table.shape[0]
    ring, rows, width = held.shape
    operands = [table, sums, held] + ([] if update is None else [update])
    return pl.pallas_call(
        functools.partial(place_kernel, blocks),
        out_shape=jax.ShapeDtypeStruct((rows, blocks * width), jnp.float32),
        in_specs=[
            pl.BlockSpec(memory_space=pltpu.SMEM),
            pl.BlockSpec(memory_space=pltpu.VMEM),
            pl.BlockSpec(memory_space=pltpu.VMEM),
        ]
        + ([] if update is None else [pl.BlockSpec(memory_space=pl.ANY)]),
        out_specs=pl.BlockSpec(memory_space=pl.ANY),
        scratch_shapes=[
            pltpu.VMEM((ring, rows, width), jnp.float32),
            pltpu.SemaphoreType.DMA((ring,)),
        ],
        input_output_aliases={} if update is None else {3: 0},
        compiler_params=pltpu.CompilerParams(vmem_limit_bytes=32 * 1024 * 1024),
        cost_estimate=pl.CostEstimate(
            flops=0, bytes_accessed=2 * ring * rows * width * 4, transcendentals=0
        ),
        name="place_own" if update is None else "place_other",
    )(*operands)


def local(gradient, left_root, right_root, first_moment, second_moment, step_count, owner_table):
    rows, width = left_root.shape[1], left_root.shape[2]
    quarters, spread, ring = lax.axis_size("q"), lax.axis_size("x"), lax.axis_size("y")
    near = 2 * spread
    is_own = (jnp.arange(2, dtype=jnp.int32) == lax.axis_index("r"))[None, :, None, None]

    def spread_pair(value, got):
        shape = (spread, 2) + value.shape
        return jnp.where(
            jnp.broadcast_to(is_own, shape),
            jnp.broadcast_to(value, shape),
            jnp.broadcast_to(got, shape),
        )

    grad = pick(owner_table, gradient, width)
    grad_pair = spread_pair(grad, shifted(grad, "r", 1))
    right_class = lax.all_gather(right_root[0], "q", axis=0, tiled=True)

    step_value = step_count[0].astype(jnp.float32)
    first_new = beta_one * first_moment[0] + (1.0 - beta_one) * grad
    second_new = beta_two * second_moment[0] + (1.0 - beta_two) * grad * grad
    first_fix = 1.0 - jnp.power(beta_one, step_value)
    second_fix = 1.0 - jnp.power(beta_two, step_value)
    adam_step = first_new / first_fix / (jnp.sqrt(second_new / second_fix) + adam_eps)
    adam_sq = jnp.sum(adam_step * adam_step)

    left_got = shifted(left_root[0], "r", 1)
    grad_pair, left_got, adam_sq = lax.optimization_barrier((grad_pair, left_got, adam_sq))
    grad_rows = exchange(grad_pair, "x")
    grad_rows = jnp.transpose(grad_rows, (1, 0, 2, 3)).reshape(near * rows, width)
    left_pair = spread_pair(left_root[0], left_got)
    left_pair, grad_rows, right_class = lax.optimization_barrier(
        (left_pair, grad_rows, right_class)
    )
    left_rows = exchange(left_pair, "x")
    right_side = lax.dot_general(
        grad_rows, right_class, (((1,), (1,)), ((), ())), precision=HIGHEST
    )
    right_all = lax.all_gather(right_side, "q", axis=0, tiled=True)
    sent = left_multiply(left_rows, right_all, adam_sq.reshape(1, 1), near, rows)
    got = exchange(sent, ("r", "x"))
    near_sums = jnp.sum(got[:, rows, :], axis=0, keepdims=True)
    totals = lax.all_gather(near_sums, "q", axis=0, tiled=True)
    own = exchange(order_copies(got, quarters, spread, rows, ring, width), "y")
    totals = jnp.sum(totals, axis=0, keepdims=True)
    all_sums = lax.all_gather(totals, ("y", "core"), axis=0, tiled=True)
    own, all_sums = lax.optimization_barrier((own, all_sums))
    other = lax.ppermute(own, "core", [(0, 1), (1, 0)])
    update = place(owner_table, all_sums, own, None)
    update = place(owner_table, all_sums, other, update)
    return update, first_new[None], second_new[None]


def solution(mesh):
    fine = Mesh(mesh.devices.reshape(4, 2, 4, 8, 2), ("q", "r", "x", "y", "core"))
    near, deep = ("q", "r", "x"), ("y", "core")
    flat, owned = P(near, None), P(deep, near, None)
    return jax.shard_map(
        local,
        mesh=fine,
        in_specs=(flat, owned, owned, owned, owned, P(), P()),
        out_specs=(flat, owned, owned),
        check_vma=False,
    )
```
